32 devices in a mesh: blk: 8 (over z, core), ctr: 4 (over y, x).
Axes of the slice: x: 2, y: 2, z: 4, core: 2. Of those that a mesh axis runs over, the one named last changes fastest.
Arguments:
- integrals: float32 [8, 3200, 12800], P('blk', None, 'ctr'), may hold values from -0.078125 to 0.078125
- amplitudes: float32 [8, 12800, 128], P(None, 'ctr', 'blk'), may hold values from -6 to 6
- blockmap: int32 [8], replicated, may hold values from 0 to 7, each once
- vir_energy: float32 [320], replicated, may hold values from 0.2 to 3
- occ_energy: float32 [32], replicated, may hold values from -2 to -0.3
Outputs:
- ladder: float32 [8, 3200, 128], P('blk', 'ctr')
- increment: float32 [8, 3200, 128], P('blk', 'ctr')
The draws below stay inside these ranges and needn't reach their ends.
Inputs may be any that keep to these rules, and one draw needn't show every extreme that they name: `blockmap`: every block number appears in exactly one slot.
All inputs are finite; a program needn't handle non-finite values.
Results may differ from the reference program's by a relative error of at most 0.0003.
Values sent between devices are 32-bit elements; how exact they have to be, the bound alone decides.
No kernel may reach another device: no remote copies, remote signals or barrier semaphores. Data moves between devices by JAX's collectives and lax.ppermute only.
A program may use at most 128 MiB of HBM per device.

```python
import jax
import jax.numpy as jnp
from jax import lax

NIRR = 8
VI = 40
OI = 4
NVIR = 320
NOCC = 32
CD = 12800
IJ = 128
QB = 1
AB_BLK = 3200
N_BLK = 8


def spiked(array, stream_key, source, target, blocks, factor):
    owner, partner = [(jnp.arange(array.shape[dim]) // (array.shape[dim] // blocks)).reshape([-1 if axis == dim else 1 for axis in range(array.ndim)]) for dim in (source, target)]
    chosen = jax.random.permutation(stream_key, blocks)[partner]
    strong = (owner == chosen) | (owner == (partner + blocks // 2) % blocks)
    return jnp.where(strong, factor * array, array)


def block_scale(key, extent, pieces, least, high):
    gain, own = 1.0, jax.random.fold_in(key, 6)
    for axis_at, parts in pieces:
        steps = jnp.exp(jax.random.uniform(jax.random.fold_in(own, axis_at), (parts,), jnp.float32, least / len(pieces), high / len(pieces)))
        gain = gain * jnp.repeat(steps, extent[axis_at] // parts).reshape([-1 if axis == axis_at else 1 for axis in range(len(extent))])
    return gain


def centred(stream_key, extent, width, reach, split=(), kind=jnp.bfloat16):
    drawn = width * jax.random.normal(stream_key, extent, jnp.float32)
    if split:
        drawn = drawn * block_scale(stream_key, extent, split, -0.22, 0.18)
    return jnp.clip(drawn, -reach, reach).astype(kind)


def noise_with(own_key, extent, deviation, most, cuts, heavy, kind=jnp.bfloat16):
    array = deviation * jax.random.normal(own_key, extent, jnp.float32)
    if cuts:
        array = array * block_scale(own_key, extent, cuts, -0.22, 0.18)
    return jnp.clip(spiked(array, jax.random.fold_in(own_key, 3), *heavy), -most, most).astype(kind)


def setup_inputs(seed: int = 0) -> dict:
    keys = jax.random.split(jax.random.key(seed), 6)
    integrals = noise_with(keys[0], (N_BLK, AB_BLK, CD), CD ** -0.5, 0.078125, ((0, 8), (2, 4)), (2, 1, 4, 2.0), jnp.float32)
    amplitudes = centred(keys[1], (NIRR, CD, IJ), 1.0, 6.0, ((1, 4), (2, 8)), jnp.float32)
    blockmap = jax.random.permutation(keys[2], N_BLK).astype(jnp.int32)
    vir_energy = jnp.clip(jax.random.uniform(keys[3], (NVIR,), jnp.float32, 0.2, 3.0), 0.2, 3.0)
    occ_energy = jnp.clip(jax.random.uniform(keys[4], (NOCC,), jnp.float32, -2.0, -0.3), -2.0, -0.3)
    return dict(integrals=integrals, amplitudes=amplitudes, blockmap=blockmap, vir_energy=vir_energy, occ_energy=occ_energy)


def denominator(block, start, count, vir_energy, occ_energy):
    irrep = block // QB
    rows = (block % QB) * AB_BLK + start + jnp.arange(count, dtype=jnp.int32)
    arow = rows // (VI * VI)
    first = arow * VI + (rows // VI) % VI
    second = jnp.bitwise_xor(arow, irrep) * VI + rows % VI
    cols = jnp.arange(IJ, dtype=jnp.int32)
    orow = cols // (OI * OI)
    hole_one = orow * OI + (cols // OI) % OI
    hole_two = jnp.bitwise_xor(orow, irrep) * OI + cols % OI
    upper = vir_energy[first] + vir_energy[second]
    lower = occ_energy[hole_one] + occ_energy[hole_two]
    return upper[:, None] - lower[None, :]


def reference(integrals, amplitudes, blockmap, vir_energy, occ_energy):
    def single(pair):
        block_ints, block = pair
        amps = amplitudes[block // QB]
        product = jnp.dot(block_ints, amps, preferred_element_type=jnp.float32, precision=lax.Precision.HIGHEST)
        denom = denominator(block, 0, AB_BLK, vir_energy, occ_energy)
        return product, product / denom

    ladder, increment = lax.map(single, (integrals, blockmap))
    return ladder, increment
```

```python
import functools

import jax
import jax.numpy as jnp
from jax import lax
from jax.experimental import pallas as pl
from jax.experimental.pallas import tpu as pltpu
from jax.sharding import PartitionSpec as P

NIRR = 8
VI = 40
OI = 4
F32 = jnp.float32
BF16 = jnp.bfloat16
ANY = pl.BlockSpec(memory_space=pl.ANY)
PREP_MIB = 4
NEAR_MIB = 9
FAR_MIB = 6
SMEM = pl.BlockSpec(memory_space=pltpu.SMEM)
HBM = pl.BlockSpec(memory_space=pltpu.HBM)
VMEM = pl.BlockSpec(memory_space=pltpu.VMEM)
NEAR = (0, 1, 2, 3)
FAR = (4, 5, 6, 7)
RING = 2


def cost(flops, nbytes):
    return pl.CostEstimate(flops=1, bytes_accessed=1, transcendentals=0)


def params(mib):
    return pltpu.CompilerParams(vmem_limit_bytes=mib * 1024 * 1024)


def denominator(block, groups, ab_block, start, count, columns, vir_energy, occ_energy):
    irrep = block // groups
    rows = block % groups * ab_block + start + jnp.arange(count, dtype=jnp.int32)
    arow = rows // (VI * VI)
    first = arow * VI + rows // VI % VI
    second = jnp.bitwise_xor(arow, irrep) * VI + rows % VI
    cols = jnp.arange(columns, dtype=jnp.int32)
    orow = cols // (OI * OI)
    hole_one = orow * OI + cols // OI % OI
    hole_two = jnp.bitwise_xor(orow, irrep) * OI + cols % OI
    upper = jnp.take(vir_energy, first) + jnp.take(vir_energy, second)
    lower = jnp.take(occ_energy, hole_one) + jnp.take(occ_energy, hole_two)
    return upper[:, None] - lower[None, :]


def general(integrals, amplitudes, blockmap, vir_energy, occ_energy):
    blocks = lax.axis_size("blk")
    groups = blocks // NIRR
    block = blockmap[lax.axis_index("blk")]
    local = integrals[0]
    ab_block = local.shape[0]
    share = ab_block // lax.axis_size("ctr")
    wanted = jnp.take(amplitudes, blockmap // groups, axis=0)
    parts = lax.all_to_all(wanted, "blk", 0, 0)
    chosen = jnp.moveaxis(parts, 0, 1).reshape(parts.shape[1], -1)
    partial_value = jnp.dot(local, chosen, preferred_element_type=F32, precision=lax.Precision.HIGHEST)
    mine = lax.psum_scatter(partial_value, "ctr", scatter_dimension=0, tiled=True)
    offset = lax.axis_index("ctr") * share
    denom = denominator(block, groups, ab_block, offset, share, mine.shape[1], vir_energy, occ_energy)
    return (mine[None], (mine / denom)[None])


def prep_kernel(messages, bm, amps, *refs):
    outs, sem = refs[:-1], refs[-1]
    me = lax.axis_index("blk")
    copies = [
        pltpu.make_async_copy(amps.at[bm[jnp.bitwise_xor(me, s)], :, pl.ds(k0, kc)], out, sem.at[n])
        for n, ((s, k0, kc), out) in enumerate(zip(messages, outs))
    ]
    for c in copies:
        c.start()
    for c in copies:
        c.wait()


def prep(blockmap, amps, messages):
    return pl.pallas_call(
        functools.partial(prep_kernel, messages),
        out_shape=[jax.ShapeDtypeStruct((amps.shape[1], kc), F32) for _, _, kc in messages],
        in_specs=[SMEM, HBM],
        out_specs=[VMEM] * len(messages),
        scratch_shapes=[pltpu.SemaphoreType.DMA((len(messages),))],
        compiler_params=params(PREP_MIB),
        cost_estimate=cost(0, 2 * 4 * amps.size),
        name="prep",
    )(blockmap, amps)


def split(x):
    hi = x.astype(BF16)
    return hi, (x - hi.astype(F32)).astype(BF16)


def weights(pieces, partners, starts, kc):
    me = lax.axis_index("blk")
    slot = [jnp.bitwise_and(jnp.bitwise_xor(me, s), 3) for s in partners]
    rows = []
    for q in range(4):
        held = [piece[:, k : k + kc] for piece, k in zip(pieces, starts)]
        x = held[3]
        for n in range(3):
            x = jnp.where(slot[n] == q, held[n], x)
        rows.append(x)
    hi, lo = split(jnp.concatenate(rows, 0).T)
    return jnp.concatenate([hi, lo], 1)


def fold(wide):
    value = wide + pltpu.roll(wide, 64, 1)
    half = value.shape[0] // 2
    left = lax.broadcasted_iota(jnp.int32, (half, 128), 1) < 64
    return jnp.where(left, value[:half], value[half:])


def near_kernel(k0, kc, starts, last, with_old, a, *refs):
    refs = list(refs)
    pieces = [refs.pop(0) for _ in NEAR]
    old = refs.pop(0) if with_old else None
    his, los = refs.pop(0), refs.pop(0)
    outs = [refs.pop(0) for _ in range(4 if last else 1)]
    buf, w, acc, sem = refs
    ctr = lax.axis_index("ctr")
    share = a.shape[0] // 4

    def load(n):
        return pltpu.make_async_copy(
            a.at[pl.ds(n * share, share), pl.ds(k0, kc)], buf.at[lax.rem(n, RING)], sem.at[lax.rem(n, RING)]
        )

    for n in range(RING):
        load(n).start()
    w[...] = weights(pieces, NEAR, starts, kc)
    sums = acc if last else outs[0]

    @pl.loop(0, 4)
    def _(t):
        load(t).wait()
        at = pl.ds(t * share, share)
        hi, lo = split(buf[lax.rem(t, RING)])
        his[at, :] = hi
        los[at, :] = lo

        @pl.when(t + RING < 4)
        def _():
            load(t + RING).start()

        wide = jnp.dot(his[at, :], w[...], preferred_element_type=F32)
        x = fold(wide + jnp.dot(los[at, :], w[...], preferred_element_type=F32))
        sums[t] = x + old[t] if with_old else x

    if last:
        for s in range(4):
            outs[s][...] = acc[jnp.bitwise_xor(ctr, s)]


def near_tile(a, span, pieces, old, last):
    k0, kc = span
    starts = [k0 - held for held, _ in pieces]
    rows = a.shape[0]
    kept = jax.ShapeDtypeStruct((rows, kc), BF16)
    packed = (rows // 8, 128)
    given = [x for _, x in pieces] + ([old] if old is not None else [])
    sums = [jax.ShapeDtypeStruct(packed, F32)] * 4 if last else [jax.ShapeDtypeStruct((4, *packed), F32)]
    out = pl.pallas_call(
        functools.partial(near_kernel, k0, kc, starts, last, old is not None),
        out_shape=[kept, kept, *sums],
        in_specs=[ANY] + [VMEM] * len(given),
        out_specs=[VMEM] * (2 + len(sums)),
        scratch_shapes=[
            pltpu.VMEM((RING, rows // 4, kc), F32),
            pltpu.VMEM((kc, 128), BF16),
            pltpu.VMEM((4, *packed), F32),
            pltpu.SemaphoreType.DMA((RING,)),
        ],
        compiler_params=params(NEAR_MIB),
        cost_estimate=cost(2 * 2 * rows * kc * 256, 4 * rows * kc),
        name="near",
    )(a, *given)
    return out[:2], (out[2:] if last else out[2])


def far_kernel(spans, s, first, *refs):
    refs = list(refs)
    kept = [(refs.pop(0), refs.pop(0)) for _ in spans]
    if first:
        pieces = [refs.pop(0) for _ in FAR]
        out, w = refs
        for k0, kc in spans:
            w[k0 : k0 + kc, :] = weights(pieces, FAR, [k0] * 4, kc)
    else:
        w, out = refs
    share = out.shape[0] * 2
    at = pl.ds(pl.multiple_of(jnp.bitwise_xor(lax.axis_index("ctr"), s) * share, share), share)
    wide = jnp.zeros((share, 128), F32)
    for (k0, kc), (hi, lo) in zip(spans, kept):
        part = w[k0 : k0 + kc, :]
        wide = wide + jnp.dot(hi[at, :], part, preferred_element_type=F32)
        wide = wide + jnp.dot(lo[at, :], part, preferred_element_type=F32)
    out[...] = fold(wide)


def far_tile(spans, kept, s, pieces=None, w=None):
    rows = kept[0][0].shape[0]
    cd = sum(kc for _, kc in spans)
    given = [x for pair in kept for x in pair] + ([w] if pieces is None else [*pieces])
    out = [jax.ShapeDtypeStruct((rows // 8, 128), F32)]
    if pieces is not None:
        out.append(jax.ShapeDtypeStruct((cd, 128), BF16))
    return pl.pallas_call(
        functools.partial(far_kernel, spans, s, pieces is not None),
        out_shape=out,
        in_specs=[VMEM] * len(given),
        out_specs=[VMEM] * len(out),
        compiler_params=params(FAR_MIB),
        cost_estimate=cost(2 * 2 * rows // 4 * cd * 256, 4 * rows // 4 * cd),
        name="far",
    )(*given)

def denom_kernel(count, bm, vir, occ, out):
    irrep = bm[lax.axis_index("blk")]
    start = lax.axis_index("ctr") * count
    vir_at = lax.broadcasted_iota(jnp.int32, (count, vir.shape[1]), 1)
    rows = start + lax.broadcasted_iota(jnp.int32, (count, vir.shape[1]), 0)
    arow = rows // (VI * VI)
    first = arow * VI + rows // VI % VI
    second = jnp.bitwise_xor(arow, irrep) * VI + rows % VI
    energy = jnp.broadcast_to(vir[...], vir_at.shape)
    pick = lambda at: jnp.sum(jnp.where(vir_at == at, energy, 0.0), axis=1, keepdims=True)
    upper = pick(first) + pick(second)
    occ_at = lax.broadcasted_iota(jnp.int32, (occ.shape[0], 128), 0)
    cols = lax.broadcasted_iota(jnp.int32, (occ.shape[0], 128), 1)
    orow = cols // (OI * OI)
    hole_one = orow * OI + cols // OI % OI
    hole_two = jnp.bitwise_xor(orow, irrep) * OI + cols % OI
    level = jnp.broadcast_to(occ[...], occ_at.shape)
    find = lambda at: jnp.sum(jnp.where(occ_at == at, level, 0.0), axis=0, keepdims=True)
    lower = find(hole_one) + find(hole_two)
    out[...] = upper - lower


def denominators(blockmap, vir_energy, occ_energy, count):
    return pl.pallas_call(
        functools.partial(denom_kernel, count),
        out_shape=jax.ShapeDtypeStruct((count, 128), F32),
        in_specs=[SMEM, VMEM, VMEM],
        out_specs=VMEM,
        compiler_params=params(8),
        cost_estimate=cost(count * 320 * 8, count * 128 * 4),
        name="denominators",
    )(blockmap, vir_energy.reshape(1, -1), occ_energy.reshape(-1, 1))


def add_kernel(*refs):
    refs[4][...] = (refs[0][...] + refs[1][...]) + (refs[2][...] + refs[3][...])


def add(parts):
    x = parts[0]
    return pl.pallas_call(
        add_kernel,
        out_shape=jax.ShapeDtypeStruct(x.shape, F32),
        in_specs=[VMEM] * 4,
        out_specs=VMEM,
        compiler_params=params(8),
        cost_estimate=cost(4 * x.size, 20 * x.size),
        name="add",
    )(*parts)


def finish_kernel(near, *refs):
    far, denom, ladder, inc = refs[:4], *refs[4:]
    low = lax.axis_index("blk") // 4 == 0
    near = near[...]
    far = (far[0][...] + far[1][...]) + (far[2][...] + far[3][...])
    one, two = jnp.where(low, near, far), jnp.where(low, far, near)
    rows = near.shape[0]
    left = lax.broadcasted_iota(jnp.int32, (rows, 128), 1) < 64
    values = (jnp.where(left, one, pltpu.roll(two, 64, 1)), jnp.where(left, pltpu.roll(one, 64, 1), two))
    for n, value in enumerate(values):
        at = slice(n * rows, (n + 1) * rows)
        ladder[0, at] = value
        inc[0, at] = value / denom[at]


def finish(near, far, denom):
    out = jax.ShapeDtypeStruct((1, *denom.shape), F32)
    return pl.pallas_call(
        finish_kernel,
        out_shape=[out, out],
        in_specs=[VMEM] * 6,
        out_specs=[VMEM] * 2,
        compiler_params=params(8),
        cost_estimate=cost(denom.size * 8, denom.size * 4 * 7),
        name="finish",
    )(near, *far, denom)


def swap(x, axis, s):
    n = lax.axis_size(axis)
    return lax.ppermute(x, axis, [(i, i ^ s) for i in range(n)])


def after(x, *first):
    return lax.optimization_barrier((x, *first))[0]


def ranges(total, parts):
    tiles = total // 128
    edges = [n * tiles // parts * 128 for n in range(parts + 1)]
    return [(a, b - a) for a, b in zip(edges, edges[1:])]


def special(integrals, amplitudes, blockmap, vir_energy, occ_energy):
    a = integrals[0]
    amps = jnp.swapaxes(amplitudes, 1, 2)
    spans = ranges(amps.shape[2], 4)
    cd = amps.shape[2]
    cut = spans[2][0]
    halves = ((0, cut), (cut, cd - cut))
    messages = [(0, 0, cd), (1, 0, cd)] + [(s, *half) for half in halves for s in (2, 3)] + [(s, 0, cd) for s in FAR]
    sends = prep(blockmap, amps, messages)
    denom = denominators(blockmap, vir_energy, occ_energy, a.shape[0] // 4)
    here = [(0, sends[0]), (0, swap(sends[1], "blk", 1))]
    early = [swap(x, "blk", s) for s, x in zip((2, 3), sends[2:4])]
    late = [swap(after(x, denom, *early), "blk", s) for s, x in zip((2, 3), sends[4:6])]
    far = [swap(x, "blk", s) for s, x in zip(FAR, sends[6:10])]
    kept, sums = [], None
    for n, span in enumerate(spans):
        rest = [(0, x) for x in early] if n < 2 else [(cut, x) for x in late]
        pair, sums = near_tile(a, span, here + rest, sums, n == len(spans) - 1)
        kept.append(pair)
    near_sum = add([sums[0], *[swap(sums[s], "ctr", s) for s in (1, 2, 3)]])
    first, w = far_tile(spans, kept, 3, far)
    far_sums = {3: swap(first, "ctr", 3)}
    for s in (1, 2, 0):
        x = far_tile(spans, kept, s, None, w if s else after(w, near_sum))[0]
        far_sums[s] = swap(x, "ctr", s) if s else x
    return tuple(finish(near_sum, [far_sums[s] for s in range(4)], denom))


def on_device(integrals, amplitudes, *rest):
    _, rows, cd = integrals.shape
    fits = (
        lax.axis_size("blk") == NIRR
        and lax.axis_size("ctr") == 4
        and rows % 128 == 0
        and cd % 128 == 0
        and amplitudes.shape[2] == 16
    )
    return (special if fits else general)(integrals, amplitudes, *rest)


def solution(mesh):
    placed = (P("blk", None, "ctr"), P(None, "ctr", "blk"), P(), P(), P())
    return jax.shard_map(
        on_device,
        mesh=mesh,
        in_specs=placed,
        out_specs=(P("blk", "ctr", None), P("blk", "ctr", None)),
        check_vma=False,
    )
```

```python
import functools

import jax
import jax.numpy as jnp
from jax import lax
from jax.experimental import pallas as pl
from jax.experimental.pallas import tpu as pltpu
from jax.sharding import PartitionSpec as P

NIRR = 8
VI = 40
OI = 4
F32 = jnp.float32
BF16 = jnp.bfloat16
ANY = pl.BlockSpec(memory_space=pl.ANY)
PREP_MIB = 56
NEAR_MIB = 14
STEP = 768
COLUMNS_MIB = 5
FAR_MIB = 4
LAST_MIB = 32
SMALL_MIB = 4
SMEM = pl.BlockSpec(memory_space=pltpu.SMEM)
VMEM = pl.BlockSpec(memory_space=pltpu.VMEM)
FAR = (4, 5, 6, 7)
RING = 3


def cost(flops, nbytes):
    return pl.CostEstimate(flops=1, bytes_accessed=1, transcendentals=0)


def params(mib):
    return pltpu.CompilerParams(vmem_limit_bytes=mib * 1024 * 1024)


def denominator(block, groups, ab_block, start, count, columns, vir_energy, occ_energy):
    irrep = block // groups
    rows = block % groups * ab_block + start + jnp.arange(count, dtype=jnp.int32)
    arow = rows // (VI * VI)
    first = arow * VI + rows // VI % VI
    second = jnp.bitwise_xor(arow, irrep) * VI + rows % VI
    cols = jnp.arange(columns, dtype=jnp.int32)
    orow = cols // (OI * OI)
    hole_one = orow * OI + cols // OI % OI
    hole_two = jnp.bitwise_xor(orow, irrep) * OI + cols % OI
    upper = jnp.take(vir_energy, first) + jnp.take(vir_energy, second)
    lower = jnp.take(occ_energy, hole_one) + jnp.take(occ_energy, hole_two)
    return upper[:, None] - lower[None, :]


def general(integrals, amplitudes, blockmap, vir_energy, occ_energy):
    blocks = lax.axis_size("blk")
    groups = blocks // NIRR
    block = blockmap[lax.axis_index("blk")]
    local = integrals[0]
    ab_block = local.shape[0]
    share = ab_block // lax.axis_size("ctr")
    wanted = jnp.take(amplitudes, blockmap // groups, axis=0)
    parts = lax.all_to_all(wanted, "blk", 0, 0)
    chosen = jnp.moveaxis(parts, 0, 1).reshape(parts.shape[1], -1)
    partial_value = jnp.dot(local, chosen, preferred_element_type=F32, precision=lax.Precision.HIGHEST)
    mine = lax.psum_scatter(partial_value, "ctr", scatter_dimension=0, tiled=True)
    offset = lax.axis_index("ctr") * share
    denom = denominator(block, groups, ab_block, offset, share, mine.shape[1], vir_energy, occ_energy)
    return (mine[None], (mine / denom)[None])


def prep_kernel(bm, amps, *refs):
    near, far, sem = refs[0], refs[1:5], refs[5]
    me = lax.axis_index("blk")
    copies = [(amps.at[bm[jnp.bitwise_or(jnp.bitwise_and(me, 4), m)]], near.at[m]) for m in range(4)]
    copies += [(amps.at[bm[jnp.bitwise_xor(me, s)]], out) for s, out in zip(FAR, far)]
    copies = [pltpu.make_async_copy(x, y, sem.at[n]) for n, (x, y) in enumerate(copies)]
    for c in copies:
        c.start()
    for c in copies:
        c.wait()


def prep(blockmap, amps):
    one = amps.shape[1:]
    out = pl.pallas_call(
        prep_kernel,
        out_shape=[jax.ShapeDtypeStruct((4, *one), F32)] + [jax.ShapeDtypeStruct(one, F32)] * 4,
        in_specs=[SMEM, ANY],
        out_specs=[VMEM] * 5,
        scratch_shapes=[pltpu.SemaphoreType.DMA((8,))],
        compiler_params=params(PREP_MIB),
        cost_estimate=cost(0, 2 * 4 * amps.size),
        name="prep",
    )(blockmap, amps)
    return out[0], out[1:]


def split(x):
    hi = x.astype(BF16)
    return hi, (x - hi.astype(F32)).astype(BF16)


def columns(sources):
    hi, lo = split(jnp.concatenate(sources, 0).T)
    return jnp.concatenate([hi, lo], 1)


def columns_kernel(*refs):
    pieces, w = refs[:4], refs[4]
    source = [jnp.bitwise_and(jnp.bitwise_xor(lax.axis_index("blk"), s), 3) for s in FAR]
    sources = []
    for q in range(4):
        x = pieces[3][...]
        for n in range(3):
            x = jnp.where(source[n] == q, pieces[n][...], x)
        sources.append(x)
    w[...] = columns(sources)


def columns_of(pieces):
    return pl.pallas_call(
        columns_kernel,
        out_shape=jax.ShapeDtypeStruct((pieces[0].shape[1], 128), BF16),
        in_specs=[VMEM] * 4,
        out_specs=VMEM,
        compiler_params=params(COLUMNS_MIB),
        cost_estimate=cost(0, 0),
        name="columns",
    )(*pieces)


def fold(wide):
    value = wide + pltpu.roll(wide, 64, 1)
    half = value.shape[0] // 2
    left = lax.broadcasted_iota(jnp.int32, (half, 128), 1) < 64
    return jnp.where(left, value[:half], value[half:])


def near_kernel(spans, a, piece, his, los, *refs):
    outs, (buf, w, last, acc, sem) = refs[:4], refs[4:]
    ctr = lax.axis_index("ctr")
    share = a.shape[0] // 4

    def load(n, s):
        k0, kc = spans[n]
        at = lax.rem(4 * n + s, RING)
        row = pl.multiple_of(jnp.bitwise_xor(ctr, 3 - s) * share, share)
        return pltpu.make_async_copy(
            a.at[pl.ds(row, share), pl.ds(k0, kc)], buf.at[at, :, pl.ds(0, kc)], sem.at[at]
        )

    for s in range(RING):
        load(0, s).start()
    for k0, kc in spans:
        w[k0 : k0 + kc, :] = columns([piece[m, :, k0 : k0 + kc] for m in range(4)])
    for n, (k0, kc) in enumerate(spans):
        cols = slice(k0, k0 + kc)

        def step(s, keep_hi, keep_lo, at, wide_cols):
            load(n, s).wait()
            hi, lo = split(buf[lax.rem(4 * n + s, RING), :, :kc])
            keep_hi[at, wide_cols] = hi
            keep_lo[at, wide_cols] = lo

            @pl.when(s + RING < 4)
            def _():
                load(n, s + RING).start()

            if n + 1 < len(spans):

                @pl.when(s + RING >= 4)
                def _():
                    load(n + 1, s + RING - 4).start()

            wide = jnp.dot(keep_hi[at, wide_cols], w[cols, :], preferred_element_type=F32)
            return fold(wide + jnp.dot(keep_lo[at, wide_cols], w[cols, :], preferred_element_type=F32))

        @pl.loop(0, 3)
        def _(s):
            x = step(s, his, los, pl.ds(pl.multiple_of(s * share, share), share), cols)
            acc[s] = acc[s] + x if n else x

        x = step(3, last.at[0], last.at[1], slice(None), slice(0, kc))
        outs[0][...] = outs[0][...] + x if n else x

    for s in range(3):
        outs[3 - s][...] = acc[s]

def near_pass(a, piece):
    rows, cd = a.shape
    spans = [(k0, min(STEP, cd - k0)) for k0 in range(0, cd, STEP)]
    kept = jax.ShapeDtypeStruct((rows // 4 * 3, cd), BF16)
    packed = (rows // 8, 128)
    widest = max(kc for _, kc in spans)
    out = pl.pallas_call(
        functools.partial(near_kernel, spans),
        out_shape=[kept, kept] + [jax.ShapeDtypeStruct(packed, F32)] * 4,
        in_specs=[ANY, VMEM],
        out_specs=[VMEM] * 6,
        scratch_shapes=[
            pltpu.VMEM((RING, rows // 4, widest), F32),
            pltpu.VMEM((cd, 128), BF16),
            pltpu.VMEM((2, rows // 4, widest), BF16),
            pltpu.VMEM((3, *packed), F32),
            pltpu.SemaphoreType.DMA((RING,)),
        ],
        compiler_params=params(NEAR_MIB),
        cost_estimate=cost(0, 0),
        name="near",
    )(a, piece)
    return out[:2], out[2:]


def far_kernel(s, hi, lo, w, out):
    share = out.shape[0] * 2
    at = slice((3 - s) * share, (4 - s) * share)
    wide = jnp.dot(hi[at, :], w[...], preferred_element_type=F32)
    out[...] = fold(wide + jnp.dot(lo[at, :], w[...], preferred_element_type=F32))


def far_tile(kept, s, w):
    rows = kept[0].shape[0]
    return pl.pallas_call(
        functools.partial(far_kernel, s),
        out_shape=jax.ShapeDtypeStruct((rows // 6, 128), F32),
        in_specs=[VMEM] * 3,
        out_specs=VMEM,
        compiler_params=params(FAR_MIB),
        cost_estimate=cost(0, 0),
        name="far",
    )(*kept, w)


def last_kernel(spans, a, w, out, buf, wide, sem):
    share = buf.shape[0]
    row = pl.multiple_of(lax.axis_index("ctr") * share, share)
    loads = [
        pltpu.make_async_copy(a.at[pl.ds(row, share), pl.ds(*span)], buf.at[:, pl.ds(*span)], sem.at[n])
        for n, span in enumerate(spans)
    ]
    for x in loads:
        x.start()
    for n, (x, (k0, kc)) in enumerate(zip(loads, spans)):
        x.wait()
        hi, lo = split(buf[:, k0 : k0 + kc])
        part = jnp.dot(hi, w[k0 : k0 + kc, :], preferred_element_type=F32)
        part = part + jnp.dot(lo, w[k0 : k0 + kc, :], preferred_element_type=F32)
        wide[...] = wide[...] + part if n else part
    out[...] = fold(wide[...])


def last_tile(a, w):
    rows, cd = a.shape
    spans = ranges(cd, 6)
    return pl.pallas_call(
        functools.partial(last_kernel, spans),
        out_shape=jax.ShapeDtypeStruct((rows // 8, 128), F32),
        in_specs=[ANY, VMEM],
        out_specs=VMEM,
        scratch_shapes=[
            pltpu.VMEM((rows // 4, cd), F32),
            pltpu.VMEM((rows // 4, 128), F32),
            pltpu.SemaphoreType.DMA((len(spans),)),
        ],
        compiler_params=params(LAST_MIB),
        cost_estimate=cost(0, 0),
        name="last",
    )(a, w)


def denom_kernel(count, bm, vir, occ, out):
    irrep = bm[lax.axis_index("blk")]
    start = lax.axis_index("ctr") * count
    vir_at = lax.broadcasted_iota(jnp.int32, (count, vir.shape[1]), 1)
    rows = start + lax.broadcasted_iota(jnp.int32, (count, vir.shape[1]), 0)
    arow = rows // (VI * VI)
    first = arow * VI + rows // VI % VI
    second = jnp.bitwise_xor(arow, irrep) * VI + rows % VI
    energy = jnp.broadcast_to(vir[...], vir_at.shape)
    pick = lambda at: jnp.sum(jnp.where(vir_at == at, energy, 0.0), axis=1, keepdims=True)
    upper = pick(first) + pick(second)
    occ_at = lax.broadcasted_iota(jnp.int32, (occ.shape[0], 128), 0)
    cols = lax.broadcasted_iota(jnp.int32, (occ.shape[0], 128), 1)
    orow = cols // (OI * OI)
    hole_one = orow * OI + cols // OI % OI
    hole_two = jnp.bitwise_xor(orow, irrep) * OI + cols % OI
    level = jnp.broadcast_to(occ[...], occ_at.shape)
    find = lambda at: jnp.sum(jnp.where(occ_at == at, level, 0.0), axis=0, keepdims=True)
    lower = find(hole_one) + find(hole_two)
    out[...] = upper - lower


def denominators(blockmap, vir_energy, occ_energy, count):
    return pl.pallas_call(
        functools.partial(denom_kernel, count),
        out_shape=jax.ShapeDtypeStruct((count, 128), F32),
        in_specs=[SMEM, VMEM, VMEM],
        out_specs=VMEM,
        compiler_params=params(8),
        cost_estimate=cost(count * 320 * 8, count * 128 * 4),
        name="denominators",
    )(blockmap, vir_energy.reshape(1, -1), occ_energy.reshape(-1, 1))


def add_kernel(*refs):
    refs[4][...] = (refs[0][...] + refs[1][...]) + (refs[2][...] + refs[3][...])


def add(parts):
    x = parts[0]
    return pl.pallas_call(
        add_kernel,
        out_shape=jax.ShapeDtypeStruct(x.shape, F32),
        in_specs=[VMEM] * 4,
        out_specs=VMEM,
        compiler_params=params(SMALL_MIB),
        cost_estimate=cost(4 * x.size, 20 * x.size),
        name="add",
    )(*parts)


def finish_kernel(near, *refs):
    far, denom, ladder, inc = refs[:4], *refs[4:]
    low = lax.axis_index("blk") // 4 == 0
    near = near[...]
    far = (far[0][...] + far[1][...]) + (far[2][...] + far[3][...])
    one, two = jnp.where(low, near, far), jnp.where(low, far, near)
    rows = near.shape[0]
    left = lax.broadcasted_iota(jnp.int32, (rows, 128), 1) < 64
    values = (jnp.where(left, one, pltpu.roll(two, 64, 1)), jnp.where(left, pltpu.roll(one, 64, 1), two))
    for n, value in enumerate(values):
        at = slice(n * rows, (n + 1) * rows)
        ladder[0, at] = value
        inc[0, at] = value / denom[at]


def finish(near, far, denom):
    out = jax.ShapeDtypeStruct((1, *denom.shape), F32)
    return pl.pallas_call(
        finish_kernel,
        out_shape=[out, out],
        in_specs=[VMEM] * 6,
        out_specs=[VMEM] * 2,
        compiler_params=params(8),
        cost_estimate=cost(denom.size * 8, denom.size * 4 * 7),
        name="finish",
    )(near, *far, denom)


def swap(x, axis, s):
    n = lax.axis_size(axis)
    return lax.ppermute(x, axis, [(i, i ^ s) for i in range(n)])


def after(x, *first):
    return lax.optimization_barrier((x, *first))[0]


def ranges(total, parts):
    tiles = total // 128
    edges = [n * tiles // parts * 128 for n in range(parts + 1)]
    return [(a, b - a) for a, b in zip(edges, edges[1:])]


def special(integrals, amplitudes, blockmap, vir_energy, occ_energy):
    a = integrals[0]
    amps = jnp.swapaxes(amplitudes, 1, 2)
    to_near, to_far = prep(blockmap, amps)
    near = lax.all_to_all(to_near, "blk", 0, 0, axis_index_groups=[[0, 1, 2, 3], [4, 5, 6, 7]])
    denom = denominators(blockmap, vir_energy, occ_energy, a.shape[0] // 4)
    far = [swap(after(x, denom), "blk", s) for s, x in zip(FAR, to_far)]
    kept, sums = near_pass(a, near)
    near_sum = add([sums[0], *[swap(sums[s], "ctr", s) for s in (1, 2, 3)]])
    w = columns_of(far)
    far_sums = {}
    for s in (3, 1, 2):
        mine = far_tile(kept, s, w)
        far_sums[s] = swap(mine, "ctr", s)
    far_sums[0] = last_tile(a, after(w, near_sum, far_sums[3], mine))
    return tuple(finish(near_sum, [far_sums[s] for s in range(4)], denom))


def on_device(integrals, amplitudes, *rest):
    _, rows, cd = integrals.shape
    fits = (
        lax.axis_size("blk") == NIRR
        and lax.axis_size("ctr") == 4
        and rows % 128 == 0
        and cd % 128 == 0
        and amplitudes.shape[2] == 16
    )
    return (special if fits else general)(integrals, amplitudes, *rest)


def solution(mesh):
    placed = (P("blk", None, "ctr"), P(None, "ctr", "blk"), P(), P(), P())
    return jax.shard_map(
        on_device,
        mesh=mesh,
        in_specs=placed,
        out_specs=(P("blk", "ctr", None), P("blk", "ctr", None)),
        check_vma=False,
    )
```

```python
import functools

import jax
import jax.numpy as jnp
from jax import lax
from jax.experimental import pallas as pl
from jax.experimental.pallas import tpu as pltpu
from jax.sharding import PartitionSpec as P

NIRR = 8
VI = 40
OI = 4
F32 = jnp.float32
BF16 = jnp.bfloat16
ANY = pl.BlockSpec(memory_space=pl.ANY)
PREP_MIB = 56
NEAR_MIB = 14
COLUMNS_MIB = 5
FAR_MIB = 4
LAST_MIB = 32
SMALL_MIB = 4
SMEM = pl.BlockSpec(memory_space=pltpu.SMEM)
VMEM = pl.BlockSpec(memory_space=pltpu.VMEM)
FAR = (4, 5, 6, 7)
RING = 3


def cost(flops, nbytes):
    return pl.CostEstimate(flops=1, bytes_accessed=1, transcendentals=0)


def params(mib):
    return pltpu.CompilerParams(vmem_limit_bytes=mib * 1024 * 1024)


def denominator(block, groups, ab_block, start, count, columns, vir_energy, occ_energy):
    irrep = block // groups
    rows = block % groups * ab_block + start + jnp.arange(count, dtype=jnp.int32)
    arow = rows // (VI * VI)
    first = arow * VI + rows // VI % VI
    second = jnp.bitwise_xor(arow, irrep) * VI + rows % VI
    cols = jnp.arange(columns, dtype=jnp.int32)
    orow = cols // (OI * OI)
    hole_one = orow * OI + cols // OI % OI
    hole_two = jnp.bitwise_xor(orow, irrep) * OI + cols % OI
    upper = jnp.take(vir_energy, first) + jnp.take(vir_energy, second)
    lower = jnp.take(occ_energy, hole_one) + jnp.take(occ_energy, hole_two)
    return upper[:, None] - lower[None, :]


def general(integrals, amplitudes, blockmap, vir_energy, occ_energy):
    blocks = lax.axis_size("blk")
    groups = blocks // NIRR
    block = blockmap[lax.axis_index("blk")]
    local = integrals[0]
    ab_block = local.shape[0]
    share = ab_block // lax.axis_size("ctr")
    wanted = jnp.take(amplitudes, blockmap // groups, axis=0)
    parts = lax.all_to_all(wanted, "blk", 0, 0)
    chosen = jnp.moveaxis(parts, 0, 1).reshape(parts.shape[1], -1)
    partial_value = jnp.dot(local, chosen, preferred_element_type=F32, precision=lax.Precision.HIGHEST)
    mine = lax.psum_scatter(partial_value, "ctr", scatter_dimension=0, tiled=True)
    offset = lax.axis_index("ctr") * share
    denom = denominator(block, groups, ab_block, offset, share, mine.shape[1], vir_energy, occ_energy)
    return (mine[None], (mine / denom)[None])


def prep_kernel(bm, amps, *refs):
    near, far, sem = refs[0], refs[1:5], refs[5]
    me = lax.axis_index("blk")
    copies = [(amps.at[bm[jnp.bitwise_or(jnp.bitwise_and(me, 4), m)]], near.at[m]) for m in range(4)]
    copies += [(amps.at[bm[jnp.bitwise_xor(me, s)]], out) for s, out in zip(FAR, far)]
    copies = [pltpu.make_async_copy(x, y, sem.at[n]) for n, (x, y) in enumerate(copies)]
    for c in copies:
        c.start()
    for c in copies:
        c.wait()


def prep(blockmap, amps):
    one = amps.shape[1:]
    out = pl.pallas_call(
        prep_kernel,
        out_shape=[jax.ShapeDtypeStruct((4, *one), F32)] + [jax.ShapeDtypeStruct(one, F32)] * 4,
        in_specs=[SMEM, ANY],
        out_specs=[VMEM] * 5,
        scratch_shapes=[pltpu.SemaphoreType.DMA((8,))],
        compiler_params=params(PREP_MIB),
        cost_estimate=cost(0, 2 * 4 * amps.size),
        name="prep",
    )(blockmap, amps)
    return out[0], out[1:]


def split(x):
    hi = x.astype(BF16)
    return hi, (x - hi.astype(F32)).astype(BF16)


def columns(sources):
    hi, lo = split(jnp.concatenate(sources, 0).T)
    return jnp.concatenate([hi, lo], 1)


def columns_kernel(*refs):
    pieces, w = refs[:4], refs[4]
    source = [jnp.bitwise_and(jnp.bitwise_xor(lax.axis_index("blk"), s), 3) for s in FAR]
    sources = []
    for q in range(4):
        x = pieces[3][...]
        for n in range(3):
            x = jnp.where(source[n] == q, pieces[n][...], x)
        sources.append(x)
    w[...] = columns(sources)


def columns_of(pieces):
    return pl.pallas_call(
        columns_kernel,
        out_shape=jax.ShapeDtypeStruct((pieces[0].shape[1], 128), BF16),
        in_specs=[VMEM] * 4,
        out_specs=VMEM,
        compiler_params=params(COLUMNS_MIB),
        cost_estimate=cost(0, 0),
        name="columns",
    )(*pieces)


def fold(wide):
    value = wide + pltpu.roll(wide, 64, 1)
    half = value.shape[0] // 2
    left = lax.broadcasted_iota(jnp.int32, (half, 128), 1) < 64
    return jnp.where(left, value[:half], value[half:])


def near_kernel(spans, a, piece, his, los, *refs):
    outs, (buf, w, acc, sem) = refs[:4], refs[4:]
    ctr = lax.axis_index("ctr")
    share = a.shape[0] // 4

    def load(n, t):
        k0, kc = spans[n]
        at = lax.rem(4 * n + t, RING)
        row = pl.multiple_of(jnp.bitwise_xor(ctr, jnp.bitwise_and(4 - t, 3)) * share, share)
        return pltpu.make_async_copy(
            a.at[pl.ds(row, share), pl.ds(k0, kc)], buf.at[at, :, pl.ds(0, kc)], sem.at[at]
        )

    for t in range(min(RING, 4)):
        load(0, t).start()
    for k0, kc in spans:
        w[k0 : k0 + kc, :] = columns([piece[m, :, k0 : k0 + kc] for m in range(4)])
    for n, (k0, kc) in enumerate(spans):
        cols = slice(k0, k0 + kc)

        @pl.loop(0, 4)
        def _(t):
            load(n, t).wait()
            at = pl.ds(pl.multiple_of(lax.max(t - 1, 0) * share, share), share)
            hi, lo = split(buf[lax.rem(4 * n + t, RING), :, :kc])
            his[at, cols] = hi
            los[at, cols] = lo

            @pl.when(t + RING < 4)
            def _():
                load(n, t + RING).start()

            if n + 1 < len(spans):

                @pl.when(t + RING >= 4)
                def _():
                    load(n + 1, t + RING - 4).start()

            wide = jnp.dot(his[at, cols], w[cols, :], preferred_element_type=F32)
            x = fold(wide + jnp.dot(los[at, cols], w[cols, :], preferred_element_type=F32))
            acc[t] = acc[t] + x if n else x

    for s in range(4):
        outs[s][...] = acc[(4 - s) % 4]


def near_pass(a, piece):
    rows, cd = a.shape
    spans = ranges(cd, 4)
    kept = jax.ShapeDtypeStruct((rows // 4 * 3, cd), BF16)
    packed = (rows // 8, 128)
    widest = max(kc for _, kc in spans)
    out = pl.pallas_call(
        functools.partial(near_kernel, spans),
        out_shape=[kept, kept] + [jax.ShapeDtypeStruct(packed, F32)] * 4,
        in_specs=[ANY, VMEM],
        out_specs=[VMEM] * 6,
        scratch_shapes=[
            pltpu.VMEM((RING, rows // 4, widest), F32),
            pltpu.VMEM((cd, 128), BF16),
            pltpu.VMEM((4, *packed), F32),
            pltpu.SemaphoreType.DMA((RING,)),
        ],
        compiler_params=params(NEAR_MIB),
        cost_estimate=cost(0, 0),
        name="near",
    )(a, piece)
    return out[:2], out[2:]


def far_kernel(s, hi, lo, w, out):
    share = out.shape[0] * 2
    at = slice((3 - s) * share, (4 - s) * share)
    wide = jnp.dot(hi[at, :], w[...], preferred_element_type=F32)
    out[...] = fold(wide + jnp.dot(lo[at, :], w[...], preferred_element_type=F32))


def far_tile(kept, s, w):
    rows = kept[0].shape[0]
    return pl.pallas_call(
        functools.partial(far_kernel, s),
        out_shape=jax.ShapeDtypeStruct((rows // 6, 128), F32),
        in_specs=[VMEM] * 3,
        out_specs=VMEM,
        compiler_params=params(FAR_MIB),
        cost_estimate=cost(0, 0),
        name="far",
    )(*kept, w)


def last_kernel(parts, a, w, out, buf, his, los, wide, sem):
    share, kc = buf.shape[1:]
    row = pl.multiple_of(lax.axis_index("ctr") * share, share)

    def load(n):
        return pltpu.make_async_copy(a.at[pl.ds(row, share), pl.ds(n * kc, kc)], buf.at[n], sem.at[n])

    for n in range(parts):
        load(n).start()
    wide[...] = jnp.zeros_like(wide)

    @pl.loop(0, parts)
    def _(n):
        load(n).wait()
        his[...], los[...] = split(buf[n])
        part = w[pl.ds(pl.multiple_of(n * kc, kc), kc), :]
        x = jnp.dot(his[...], part, preferred_element_type=F32)
        wide[...] = wide[...] + (x + jnp.dot(los[...], part, preferred_element_type=F32))

    out[...] = fold(wide[...])


def last_tile(a, w):
    rows, cd = a.shape
    parts = 5
    kept = pltpu.VMEM((rows // 4, cd // parts), BF16)
    return pl.pallas_call(
        functools.partial(last_kernel, parts),
        out_shape=jax.ShapeDtypeStruct((rows // 8, 128), F32),
        in_specs=[ANY, VMEM],
        out_specs=VMEM,
        scratch_shapes=[
            pltpu.VMEM((parts, rows // 4, cd // parts), F32),
            kept,
            kept,
            pltpu.VMEM((rows // 4, 128), F32),
            pltpu.SemaphoreType.DMA((parts,)),
        ],
        compiler_params=params(LAST_MIB),
        cost_estimate=cost(0, 0),
        name="last",
    )(a, w)


def denom_kernel(count, bm, vir, occ, out):
    irrep = bm[lax.axis_index("blk")]
    start = lax.axis_index("ctr") * count
    vir_at = lax.broadcasted_iota(jnp.int32, (count, vir.shape[0]), 1)
    rows = start + lax.broadcasted_iota(jnp.int32, (count, vir.shape[0]), 0)
    arow = rows // (VI * VI)
    first = arow * VI + rows // VI % VI
    second = jnp.bitwise_xor(arow, irrep) * VI + rows % VI
    energy = jnp.broadcast_to(vir[...].reshape(1, -1), vir_at.shape)
    pick = lambda at: jnp.sum(jnp.where(vir_at == at, energy, 0.0), axis=1, keepdims=True)
    upper = pick(first) + pick(second)
    cols = lax.broadcasted_iota(jnp.int32, (1, 128), 1)
    orow = cols // (OI * OI)
    hole_one = orow * OI + cols // OI % OI
    hole_two = jnp.bitwise_xor(orow, irrep) * OI + cols % OI
    one, two = jnp.zeros((1, 128), F32), jnp.zeros((1, 128), F32)
    for n in range(occ.shape[0]):
        one = jnp.where(hole_one == n, occ[n], one)
        two = jnp.where(hole_two == n, occ[n], two)
    lower = one + two
    out[...] = upper - lower


def denominators(blockmap, vir_energy, occ_energy, count):
    return pl.pallas_call(
        functools.partial(denom_kernel, count),
        out_shape=jax.ShapeDtypeStruct((count, 128), F32),
        in_specs=[SMEM, VMEM, SMEM],
        out_specs=VMEM,
        compiler_params=params(8),
        cost_estimate=cost(count * 320 * 8, count * 128 * 4),
        name="denominators",
    )(blockmap, vir_energy, occ_energy)


def add_kernel(*refs):
    refs[4][...] = (refs[0][...] + refs[1][...]) + (refs[2][...] + refs[3][...])


def add(parts):
    x = parts[0]
    return pl.pallas_call(
        add_kernel,
        out_shape=jax.ShapeDtypeStruct(x.shape, F32),
        in_specs=[VMEM] * 4,
        out_specs=VMEM,
        compiler_params=params(SMALL_MIB),
        cost_estimate=cost(4 * x.size, 20 * x.size),
        name="add",
    )(*parts)


def finish_kernel(near, *refs):
    far, denom, ladder, inc = refs[:4], *refs[4:]
    low = lax.axis_index("blk") // 4 == 0
    near = near[...]
    far = (far[0][...] + far[1][...]) + (far[2][...] + far[3][...])
    one, two = jnp.where(low, near, far), jnp.where(low, far, near)
    rows = near.shape[0]
    left = lax.broadcasted_iota(jnp.int32, (rows, 128), 1) < 64
    values = (jnp.where(left, one, pltpu.roll(two, 64, 1)), jnp.where(left, pltpu.roll(one, 64, 1), two))
    for n, value in enumerate(values):
        at = slice(n * rows, (n + 1) * rows)
        ladder[0, at] = value
        inc[0, at] = value / denom[at]


def finish(near, far, denom):
    out = jax.ShapeDtypeStruct((1, *denom.shape), F32)
    return pl.pallas_call(
        finish_kernel,
        out_shape=[out, out],
        in_specs=[VMEM] * 6,
        out_specs=[VMEM] * 2,
        compiler_params=params(8),
        cost_estimate=cost(denom.size * 8, denom.size * 4 * 7),
        name="finish",
    )(near, *far, denom)


def swap(x, axis, s):
    n = lax.axis_size(axis)
    return lax.ppermute(x, axis, [(i, i ^ s) for i in range(n)])


def after(x, *first):
    return lax.optimization_barrier((x, *first))[0]


def ranges(total, parts):
    tiles = total // 128
    edges = [n * tiles // parts * 128 for n in range(parts + 1)]
    return [(a, b - a) for a, b in zip(edges, edges[1:])]


def special(integrals, amplitudes, blockmap, vir_energy, occ_energy):
    a = integrals[0]
    amps = jnp.swapaxes(amplitudes, 1, 2)
    to_near, to_far = prep(blockmap, amps)
    near = lax.all_to_all(to_near, "blk", 0, 0, axis_index_groups=[[0, 1, 2, 3], [4, 5, 6, 7]])
    denom = denominators(blockmap, vir_energy, occ_energy, a.shape[0] // 4)
    far = [swap(x, "blk", s) for s, x in zip(FAR, to_far)]
    kept, sums = near_pass(a, after(near, denom))
    near_sum = add([sums[0], *[swap(sums[s], "ctr", s) for s in (1, 2, 3)]])
    w = columns_of(far)
    far_sums = {}
    for s in (3, 1, 2):
        mine = far_tile(kept, s, w)
        far_sums[s] = swap(mine, "ctr", s)
    far_sums[0] = last_tile(a, after(w, near_sum, far_sums[3], mine))
    return tuple(finish(near_sum, [far_sums[s] for s in range(4)], denom))


def on_device(integrals, amplitudes, *rest):
    _, rows, cd = integrals.shape
    fits = (
        lax.axis_size("blk") == NIRR
        and lax.axis_size("ctr") == 4
        and rows % 128 == 0
        and cd % 640 == 0
        and amplitudes.shape[2] == 16
    )
    return (special if fits else general)(integrals, amplitudes, *rest)


def solution(mesh):
    placed = (P("blk", None, "ctr"), P(None, "ctr", "blk"), P(), P(), P())
    return jax.shard_map(
        on_device,
        mesh=mesh,
        in_specs=placed,
        out_specs=(P("blk", "ctr", None), P("blk", "ctr", None)),
        check_vma=False,
    )
```

```python
import functools

import jax
import jax.numpy as jnp
from jax import lax
from jax.experimental import pallas as pl
from jax.experimental.pallas import tpu as pltpu
from jax.sharding import PartitionSpec as P

NIRR = 8
VI = 40
OI = 4
F32 = jnp.float32
BF16 = jnp.bfloat16
ANY = pl.BlockSpec(memory_space=pl.ANY)
PREP_MIB = 56
NEAR_MIB = 14
COLUMNS_MIB = 5
FAR_MIB = 4
LAST_MIB = 32
SMALL_MIB = 4
SMEM = pl.BlockSpec(memory_space=pltpu.SMEM)
VMEM = pl.BlockSpec(memory_space=pltpu.VMEM)
FAR = (4, 5, 6, 7)
RING = 3


def cost(flops, nbytes):
    return pl.CostEstimate(flops=1, bytes_accessed=1, transcendentals=0)


def params(mib):
    return pltpu.CompilerParams(vmem_limit_bytes=mib * 1024 * 1024)


def denominator(block, groups, ab_block, start, count, columns, vir_energy, occ_energy):
    irrep = block // groups
    rows = block % groups * ab_block + start + jnp.arange(count, dtype=jnp.int32)
    arow = rows // (VI * VI)
    first = arow * VI + rows // VI % VI
    second = jnp.bitwise_xor(arow, irrep) * VI + rows % VI
    cols = jnp.arange(columns, dtype=jnp.int32)
    orow = cols // (OI * OI)
    hole_one = orow * OI + cols // OI % OI
    hole_two = jnp.bitwise_xor(orow, irrep) * OI + cols % OI
    upper = jnp.take(vir_energy, first) + jnp.take(vir_energy, second)
    lower = jnp.take(occ_energy, hole_one) + jnp.take(occ_energy, hole_two)
    return upper[:, None] - lower[None, :]


def general(integrals, amplitudes, blockmap, vir_energy, occ_energy):
    blocks = lax.axis_size("blk")
    groups = blocks // NIRR
    block = blockmap[lax.axis_index("blk")]
    local = integrals[0]
    ab_block = local.shape[0]
    share = ab_block // lax.axis_size("ctr")
    wanted = jnp.take(amplitudes, blockmap // groups, axis=0)
    parts = lax.all_to_all(wanted, "blk", 0, 0)
    chosen = jnp.moveaxis(parts, 0, 1).reshape(parts.shape[1], -1)
    partial_value = jnp.dot(local, chosen, preferred_element_type=F32, precision=lax.Precision.HIGHEST)
    mine = lax.psum_scatter(partial_value, "ctr", scatter_dimension=0, tiled=True)
    offset = lax.axis_index("ctr") * share
    denom = denominator(block, groups, ab_block, offset, share, mine.shape[1], vir_energy, occ_energy)
    return (mine[None], (mine / denom)[None])


def prep_kernel(bm, amps, *refs):
    near, far, sem = refs[0], refs[1:5], refs[5]
    me = lax.axis_index("blk")
    copies = [(amps.at[bm[jnp.bitwise_or(jnp.bitwise_and(me, 4), m)]], near.at[m]) for m in range(4)]
    copies += [(amps.at[bm[jnp.bitwise_xor(me, s)]], out) for s, out in zip(FAR, far)]
    copies = [pltpu.make_async_copy(x, y, sem.at[n]) for n, (x, y) in enumerate(copies)]
    for c in copies:
        c.start()
    for c in copies:
        c.wait()


def prep(blockmap, amps):
    one = amps.shape[1:]
    out = pl.pallas_call(
        prep_kernel,
        out_shape=[jax.ShapeDtypeStruct((4, *one), F32)] + [jax.ShapeDtypeStruct(one, F32)] * 4,
        in_specs=[SMEM, ANY],
        out_specs=[VMEM] * 5,
        scratch_shapes=[pltpu.SemaphoreType.DMA((8,))],
        compiler_params=params(PREP_MIB),
        cost_estimate=cost(0, 2 * 4 * amps.size),
        name="prep",
    )(blockmap, amps)
    return out[0], out[1:]


def split(x):
    hi = x.astype(BF16)
    return hi, (x - hi.astype(F32)).astype(BF16)


def columns(sources):
    hi, lo = split(jnp.concatenate(sources, 0).T)
    return jnp.concatenate([hi, lo], 1)


def columns_kernel(*refs):
    pieces, w = refs[:4], refs[4]
    source = [jnp.bitwise_and(jnp.bitwise_xor(lax.axis_index("blk"), s), 3) for s in FAR]
    sources = []
    for q in range(4):
        x = pieces[3][...]
        for n in range(3):
            x = jnp.where(source[n] == q, pieces[n][...], x)
        sources.append(x)
    w[...] = columns(sources)


def columns_of(pieces):
    return pl.pallas_call(
        columns_kernel,
        out_shape=jax.ShapeDtypeStruct((pieces[0].shape[1], 128), BF16),
        in_specs=[VMEM] * 4,
        out_specs=VMEM,
        compiler_params=params(COLUMNS_MIB),
        cost_estimate=cost(0, 0),
        name="columns",
    )(*pieces)


def fold(wide):
    value = wide + pltpu.roll(wide, 64, 1)
    half = value.shape[0] // 2
    left = lax.broadcasted_iota(jnp.int32, (half, 128), 1) < 64
    return jnp.where(left, value[:half], value[half:])


def near_kernel(spans, a, piece, his, los, *refs):
    outs, (buf, w, acc, sem) = refs[:4], refs[4:]
    ctr = lax.axis_index("ctr")
    share = a.shape[0] // 4

    def load(n, t):
        k0, kc = spans[n]
        at = lax.rem(4 * n + t, RING)
        row = pl.multiple_of(jnp.bitwise_xor(ctr, jnp.bitwise_and(4 - t, 3)) * share, share)
        return pltpu.make_async_copy(
            a.at[pl.ds(row, share), pl.ds(k0, kc)], buf.at[at, :, pl.ds(0, kc)], sem.at[at]
        )

    for t in range(min(RING, 4)):
        load(0, t).start()
    for k0, kc in spans:
        w[k0 : k0 + kc, :] = columns([piece[m, :, k0 : k0 + kc] for m in range(4)])
    for n, (k0, kc) in enumerate(spans):
        cols = slice(k0, k0 + kc)

        @pl.loop(0, 4)
        def _(t):
            load(n, t).wait()
            at = pl.ds(pl.multiple_of(lax.max(t - 1, 0) * share, share), share)
            hi, lo = split(buf[lax.rem(4 * n + t, RING), :, :kc])
            his[at, cols] = hi
            los[at, cols] = lo

            @pl.when(t + RING < 4)
            def _():
                load(n, t + RING).start()

            if n + 1 < len(spans):

                @pl.when(t + RING >= 4)
                def _():
                    load(n + 1, t + RING - 4).start()

            wide = jnp.dot(his[at, cols], w[cols, :], preferred_element_type=F32)
            x = fold(wide + jnp.dot(los[at, cols], w[cols, :], preferred_element_type=F32))
            acc[t] = acc[t] + x if n else x

    for s in range(4):
        outs[s][...] = acc[(4 - s) % 4]


def near_pass(a, piece):
    rows, cd = a.shape
    spans = ranges(cd, 4)
    kept = jax.ShapeDtypeStruct((rows // 4 * 3, cd), BF16)
    packed = (rows // 8, 128)
    widest = max(kc for _, kc in spans)
    out = pl.pallas_call(
        functools.partial(near_kernel, spans),
        out_shape=[kept, kept] + [jax.ShapeDtypeStruct(packed, F32)] * 4,
        in_specs=[ANY, VMEM],
        out_specs=[VMEM] * 6,
        scratch_shapes=[
            pltpu.VMEM((RING, rows // 4, widest), F32),
            pltpu.VMEM((cd, 128), BF16),
            pltpu.VMEM((4, *packed), F32),
            pltpu.SemaphoreType.DMA((RING,)),
        ],
        compiler_params=params(NEAR_MIB),
        cost_estimate=cost(0, 0),
        name="near",
    )(a, piece)
    return out[:2], out[2:]


def far_kernel(s, hi, lo, w, out):
    share = out.shape[0] * 2
    at = slice((3 - s) * share, (4 - s) * share)
    wide = jnp.dot(hi[at, :], w[...], preferred_element_type=F32)
    out[...] = fold(wide + jnp.dot(lo[at, :], w[...], preferred_element_type=F32))


def far_tile(kept, s, w):
    rows = kept[0].shape[0]
    return pl.pallas_call(
        functools.partial(far_kernel, s),
        out_shape=jax.ShapeDtypeStruct((rows // 6, 128), F32),
        in_specs=[VMEM] * 3,
        out_specs=VMEM,
        compiler_params=params(FAR_MIB),
        cost_estimate=cost(0, 0),
        name="far",
    )(*kept, w)


def last_kernel(parts, a, w, out, buf, his, los, wide, sem):
    share, kc = buf.shape[1:]
    row = pl.multiple_of(lax.axis_index("ctr") * share, share)

    def load(n):
        return pltpu.make_async_copy(a.at[pl.ds(row, share), pl.ds(n * kc, kc)], buf.at[n], sem.at[n])

    for n in range(parts):
        load(n).start()
    wide[...] = jnp.zeros_like(wide)

    @pl.loop(0, parts)
    def _(n):
        load(n).wait()
        his[...], los[...] = split(buf[n])
        part = w[pl.ds(pl.multiple_of(n * kc, kc), kc), :]
        x = jnp.dot(his[...], part, preferred_element_type=F32)
        wide[...] = wide[...] + (x + jnp.dot(los[...], part, preferred_element_type=F32))

    out[...] = fold(wide[...])


def last_tile(a, w):
    rows, cd = a.shape
    parts = 5
    kept = pltpu.VMEM((rows // 4, cd // parts), BF16)
    return pl.pallas_call(
        functools.partial(last_kernel, parts),
        out_shape=jax.ShapeDtypeStruct((rows // 8, 128), F32),
        in_specs=[ANY, VMEM],
        out_specs=VMEM,
        scratch_shapes=[
            pltpu.VMEM((parts, rows // 4, cd // parts), F32),
            kept,
            kept,
            pltpu.VMEM((rows // 4, 128), F32),
            pltpu.SemaphoreType.DMA((parts,)),
        ],
        compiler_params=params(LAST_MIB),
        cost_estimate=cost(0, 0),
        name="last",
    )(a, w)


def denom_kernel(count, bm, vir, occ, out):
    irrep = bm[lax.axis_index("blk")]
    start = lax.axis_index("ctr") * count
    vir_at = lax.broadcasted_iota(jnp.int32, (count, vir.shape[0]), 1)
    rows = start + lax.broadcasted_iota(jnp.int32, (count, vir.shape[0]), 0)
    arow = rows // (VI * VI)
    first = arow * VI + rows // VI % VI
    second = jnp.bitwise_xor(arow, irrep) * VI + rows % VI
    energy = jnp.broadcast_to(vir[...].reshape(1, -1), vir_at.shape)
    pick = lambda at: jnp.sum(jnp.where(vir_at == at, energy, 0.0), axis=1, keepdims=True)
    upper = pick(first) + pick(second)
    cols = lax.broadcasted_iota(jnp.int32, (1, 128), 1)
    orow = cols // (OI * OI)
    hole_one = orow * OI + cols // OI % OI
    hole_two = jnp.bitwise_xor(orow, irrep) * OI + cols % OI
    one, two = jnp.zeros((1, 128), F32), jnp.zeros((1, 128), F32)
    for n in range(occ.shape[0]):
        one = jnp.where(hole_one == n, occ[n], one)
        two = jnp.where(hole_two == n, occ[n], two)
    lower = one + two
    out[...] = upper - lower


def denominators(blockmap, vir_energy, occ_energy, count):
    return pl.pallas_call(
        functools.partial(denom_kernel, count),
        out_shape=jax.ShapeDtypeStruct((count, 128), F32),
        in_specs=[SMEM, VMEM, SMEM],
        out_specs=VMEM,
        compiler_params=params(8),
        cost_estimate=cost(count * 320 * 8, count * 128 * 4),
        name="denominators",
    )(blockmap, vir_energy, occ_energy)


def add_kernel(*refs):
    refs[4][...] = (refs[0][...] + refs[1][...]) + (refs[2][...] + refs[3][...])


def add(parts):
    x = parts[0]
    return pl.pallas_call(
        add_kernel,
        out_shape=jax.ShapeDtypeStruct(x.shape, F32),
        in_specs=[VMEM] * 4,
        out_specs=VMEM,
        compiler_params=params(SMALL_MIB),
        cost_estimate=cost(4 * x.size, 20 * x.size),
        name="add",
    )(*parts)


def finish_kernel(near, *refs):
    far, denom, ladder, inc = refs[:4], *refs[4:]
    low = lax.axis_index("blk") // 4 == 0
    near = near[...]
    far = (far[0][...] + far[1][...]) + (far[2][...] + far[3][...])
    one, two = jnp.where(low, near, far), jnp.where(low, far, near)
    rows = near.shape[0]
    left = lax.broadcasted_iota(jnp.int32, (rows, 128), 1) < 64
    values = (jnp.where(left, one, pltpu.roll(two, 64, 1)), jnp.where(left, pltpu.roll(one, 64, 1), two))
    for n, value in enumerate(values):
        at = slice(n * rows, (n + 1) * rows)
        ladder[0, at] = value
        inc[0, at] = value / denom[at]


def finish(near, far, denom):
    out = jax.ShapeDtypeStruct((1, *denom.shape), F32)
    return pl.pallas_call(
        finish_kernel,
        out_shape=[out, out],
        in_specs=[VMEM] * 6,
        out_specs=[VMEM] * 2,
        compiler_params=params(8),
        cost_estimate=cost(denom.size * 8, denom.size * 4 * 7),
        name="finish",
    )(near, *far, denom)


def swap(x, axis, s):
    n = lax.axis_size(axis)
    return lax.ppermute(x, axis, [(i, i ^ s) for i in range(n)])


def after(x, *first):
    return lax.optimization_barrier((x, *first))[0]


def ranges(total, parts):
    tiles = total // 128
    edges = [n * tiles // parts * 128 for n in range(parts + 1)]
    return [(a, b - a) for a, b in zip(edges, edges[1:])]


def special(integrals, amplitudes, blockmap, vir_energy, occ_energy):
    a = integrals[0]
    amps = jnp.swapaxes(amplitudes, 1, 2)
    to_near, to_far = prep(blockmap, amps)
    near = lax.all_to_all(to_near, "blk", 0, 0, axis_index_groups=[[0, 1, 2, 3], [4, 5, 6, 7]])
    denom = denominators(blockmap, vir_energy, occ_energy, a.shape[0] // 4)
    far = [swap(x, "blk", s) for s, x in zip(FAR, to_far)]
    kept, sums = near_pass(a, after(near, denom))
    near_sum = add([sums[0], *[swap(sums[s], "ctr", s) for s in (3, 1, 2)]])
    w = columns_of(far)
    far_sums = {}
    for s in (3, 1, 2):
        mine = far_tile(kept, s, w)
        far_sums[s] = swap(mine, "ctr", s)
    far_sums[0] = last_tile(a, after(w, near_sum, far_sums[3], mine))
    return tuple(finish(near_sum, [far_sums[s] for s in range(4)], denom))


def on_device(integrals, amplitudes, *rest):
    _, rows, cd = integrals.shape
    fits = (
        lax.axis_size("blk") == NIRR
        and lax.axis_size("ctr") == 4
        and rows % 128 == 0
        and cd % 640 == 0
        and amplitudes.shape[2] == 16
    )
    return (special if fits else general)(integrals, amplitudes, *rest)


def solution(mesh):
    placed = (P("blk", None, "ctr"), P(None, "ctr", "blk"), P(), P(), P())
    return jax.shard_map(
        on_device,
        mesh=mesh,
        in_specs=placed,
        out_specs=(P("blk", "ctr", None), P("blk", "ctr", None)),
        check_vma=False,
    )
```
